32 devices in a mesh: dp: 8 (over z, x), tensor: 4 (over y, core).
Axes of the slice: x: 2, y: 2, z: 4, core: 2. Of those that a mesh axis runs over, the one named last changes fastest.
Arguments:
- residual: bfloat16 [16384, 1024], P(('dp', 'tensor')), may hold values from -6 to 6
- cotangent: bfloat16 [16384, 1024], P(('dp', 'tensor')), may hold values from -6 to 6
- seq_ids: int32 [16384], P('dp'), may hold values from -1 to 15, as said below
- w_zx: bfloat16 [1024, 2, 2048], P('dp', None, 'tensor'), may hold values from -0.1875 to 0.1875
- w_bc: bfloat16 [1024, 256], P('dp'), may hold values from -0.1875 to 0.1875
- w_dt: bfloat16 [1024, 32], P('dp', 'tensor'), may hold values from -0.09375 to 0.09375
- w_out: bfloat16 [2048, 1024], P('tensor', 'dp'), may hold values from -0.125 to 0.125
- conv_weight: float32 [4, 2304], replicated, may hold values from -3 to 3
- conv_bias: float32 [2304], replicated, may hold values from -2 to 2
- dt_bias: float32 [32], replicated, may hold values from -7 to -2.5
- a_log: float32 [32], replicated, may hold values from -1.5 to 2.7
- d_skip: float32 [32], replicated, may hold values from 0.5 to 1.5
- norm_gain: float32 [2048], replicated, may hold values from 0.5 to 1.5
- pre_gain: float32 [1024], replicated, may hold values from 0.5 to 1.5
Outputs:
- output: float32 [16384, 1024], P(('dp', 'tensor'))
- grad_residual: float32 [16384, 1024], P(('dp', 'tensor'))
- grad_w_zx: float32 [1024, 2, 2048], P('dp', None, 'tensor')
- grad_w_bc: float32 [1024, 256], P('dp')
- grad_w_dt: float32 [1024, 32], P('dp', 'tensor')
- grad_w_out: float32 [2048, 1024], P('tensor', 'dp')
- grad_conv_weight: float32 [4, 2304], replicated
- grad_conv_bias: float32 [2304], replicated
- grad_dt_bias: float32 [32], replicated
- grad_a_log: float32 [32], replicated
- grad_d_skip: float32 [32], replicated
- grad_norm_gain: float32 [2048], replicated
- grad_pre_gain: float32 [1024], replicated
The draws below stay inside these ranges and needn't reach their ends.
Inputs may be any that keep to these rules, and one draw needn't show every extreme that they name: `seq_ids`: each group of 2048 consecutive rows holds one or two whole sequences of 1024 to 2048 rows each, numbered 2 k and 2 k + 1 in group k, from the group's first row on, then rows marked -1; in every draw some group holds a single sequence of all its 2048 rows.
All inputs are finite; a program needn't handle non-finite values.
Results may differ from the reference program's by a relative error of at most 0.012.
The reference program's roundings to bfloat16 on the way count: a program that leaves them out, or rounds other values in their place, can miss the bound.
Values may be sent and summed in bfloat16 or wider, within the bound.
A program may use at most 128 MiB of HBM per device.

```python
import jax
import jax.numpy as jnp
from jax import lax

D = 1024
DI = 2048
H = 32
P_SIZE = 64
NS = 128
KCONV = 4
BLOCK = 256
SEQ_MIN = 1024
GROUP = 2048
TOKENS = 16384


def draw_seq_ids(key, part):
    key = jax.random.fold_in(key, 11)
    subkeys = jax.random.split(key, 4)
    group_count = TOKENS // GROUP
    group_index = jnp.arange(group_count)
    spare_rows = jax.random.randint(subkeys[0], (group_count,), 0, GROUP - SEQ_MIN + 1)
    whole_group = jax.random.randint(subkeys[1], (), 0, group_count)
    spare_rows = jnp.where(group_index == whole_group, 0, spare_rows)
    filled_rows = GROUP - spare_rows
    upper_cut = jnp.maximum(filled_rows - SEQ_MIN + 1, SEQ_MIN + 1)
    cut_point = jax.random.randint(subkeys[2], (group_count,), SEQ_MIN, upper_cut)
    coin_flip = jax.random.randint(subkeys[3], (group_count,), 0, 2)
    has_split = (filled_rows >= 2 * SEQ_MIN) & (coin_flip == 1) & (group_index != whole_group)
    places = jnp.arange(GROUP)[None, :]
    second_seq = (has_split[:, None] & (places >= cut_point[:, None])).astype(jnp.int32)
    numbered = jnp.where(places < filled_rows[:, None], 2 * group_index[:, None] + second_seq, -1)
    return numbered.reshape(-1).astype(jnp.int32)


def level_of(rng, extent, pieces, low, high):
    def one(position, parts):
        draws = jax.random.uniform(jax.random.fold_in(jax.random.fold_in(rng, 6), position), (parts,), jnp.float32, low / len(pieces), high / len(pieces))
        return jnp.repeat(jnp.exp(draws), extent[position] // parts).reshape((-1,) + (1,) * (len(extent) - position - 1))

    level = one(*pieces[0])
    for cut in pieces[1:]:
        level = level * one(*cut)
    return level


def bell_draw(stream_key, dims, scale, limit, cuts=(), kind=jnp.bfloat16):
    level = level_of(stream_key, dims, cuts, -0.22, 0.18) if cuts else 1.0
    values = jax.random.normal(stream_key, dims, jnp.float32) * scale * level
    return jnp.minimum(jnp.maximum(values, -limit), limit).astype(kind)


def setup_inputs(seed: int = 0) -> dict:
    arg_keys = jax.random.split(jax.random.key(seed), 15)
    return {
        "residual": bell_draw(arg_keys[0], (TOKENS, D), 1.0, 6.0, ((0, 32),)),
        "cotangent": bell_draw(arg_keys[1], (TOKENS, D), 1.0, 6.0, ((0, 32),)),
        "seq_ids": draw_seq_ids(jax.random.fold_in(arg_keys[14], 71), 0),
        "w_zx": bell_draw(arg_keys[3], (D, 2, DI), D ** -0.5, 0.1875, ((0, 8), (2, 4))),
        "w_bc": bell_draw(arg_keys[4], (D, 2 * NS), D ** -0.5, 0.1875, ((0, 8),)),
        "w_dt": bell_draw(arg_keys[5], (D, H), (4 * D) ** -0.5, 0.09375, ((0, 8), (1, 4))),
        "w_out": bell_draw(arg_keys[6], (DI, D), DI ** -0.5, 0.125, ((0, 4), (1, 8))),
        "conv_weight": bell_draw(arg_keys[7], (KCONV, DI + 2 * NS), 0.5, 3.0, (), jnp.float32),
        "conv_bias": bell_draw(arg_keys[8], (DI + 2 * NS,), 0.3, 2.0, (), jnp.float32),
        "dt_bias": jnp.clip(jax.random.uniform(arg_keys[9], (H,), jnp.float32, -7.0, -2.5), -7.0, -2.5),
        "a_log": jnp.clip(jax.random.uniform(arg_keys[10], (H,), jnp.float32, -1.5, 2.7), -1.5, 2.7),
        "d_skip": jnp.clip(jax.random.uniform(arg_keys[11], (H,), jnp.float32, 0.5, 1.5), 0.5, 1.5),
        "norm_gain": jnp.clip(1.0 + 0.1 * jax.random.normal(arg_keys[12], (DI,), jnp.float32), 0.5, 1.5),
        "pre_gain": jnp.clip(1.0 + 0.1 * jax.random.normal(arg_keys[13], (D,), jnp.float32), 0.5, 1.5),
    }


EPSILON = 1e-05
HIGHEST = lax.Precision.HIGHEST

@jax.custom_vjp
def low(v):
    return lax.optimization_barrier(v.astype(jnp.bfloat16)).astype(jnp.float32)

@jax.custom_vjp
def low_back(v):
    return v

def low_keep(v):
    return (low(v), None)

def low_pass(kept, grad):
    return (grad,)

def back_keep(v):
    return (v, None)

def back_low(kept, grad):
    return (low(grad),)
low.defvjp(low_keep, low_pass)
low_back.defvjp(back_keep, back_low)

def silu_of(value):
    return value * jax.nn.sigmoid(value)

def state_scan(inputs, b_rows, c_rows, raw_rates, bias_vec, log_rates, skip_gain, row_ids, previous, state_init):
    row_count, head_count, head_dim = inputs.shape
    block_total = row_count // BLOCK
    step_size = jax.nn.softplus(raw_rates + bias_vec)
    log_decay = -jnp.exp(log_rates) * step_size
    lower_mask = jnp.arange(BLOCK)[:, None] >= jnp.arange(BLOCK)[None, :]

    def one_block(carry, block_data):
        state, last_id = carry
        block_in, block_b, block_c, block_dt, block_decay, block_ids = block_data
        cumulated = jnp.cumsum(block_decay, axis=0)
        together = (block_ids[:, None] == block_ids[None, :]) & lower_mask
        decay_gap = jnp.where(together[:, :, None], cumulated[:, None, :] - cumulated[None, :, :], 0.0)
        weights = jnp.where(together[:, :, None], jnp.exp(decay_gap), 0.0)
        scores = jnp.dot(block_c, block_b.T, precision=HIGHEST)
        mixing = scores[:, :, None] * weights * block_dt[None, :, :]
        inner_part = jnp.einsum('ijh,jhp->ihp', mixing, block_in, precision=HIGHEST)
        carried = jnp.where((block_ids == last_id)[:, None], jnp.exp(cumulated), 0.0)
        state_part = jnp.einsum('in,hpn->ihp', block_c, state, precision=HIGHEST) * carried[:, :, None]
        end_id = block_ids[-1]
        tail_weight = jnp.where((block_ids == end_id)[:, None], jnp.exp(cumulated[-1][None, :] - cumulated), 0.0) * block_dt
        kept_share = jnp.where(end_id == last_id, jnp.exp(cumulated[-1]), 0.0)
        fresh_state = jnp.einsum('jhp,jn->hpn', block_in * tail_weight[:, :, None], block_b, precision=HIGHEST)
        new_state = state * kept_share[:, None, None] + fresh_state
        block_out = inner_part + state_part + skip_gain[None, :, None] * block_in
        return ((new_state, end_id), block_out)
    block_data = (inputs.reshape(block_total, BLOCK, head_count, head_dim), b_rows.reshape(block_total, BLOCK, -1), c_rows.reshape(block_total, BLOCK, -1), step_size.reshape(block_total, BLOCK, head_count), log_decay.reshape(block_total, BLOCK, head_count), row_ids.reshape(block_total, BLOCK))
    (final_state, _), outputs = lax.scan(jax.checkpoint(one_block), (state_init, previous), block_data)
    return (outputs.reshape(row_count, head_count, head_dim), final_state, log_decay)

def group_forward(rows_in, group_ids, w_zx, w_bc, w_dt, w_out, conv_weight, conv_bias, dt_bias, a_log, d_skip, norm_gain, pre_gain):
    mean_sq = lax.optimization_barrier(jnp.mean(rows_in * rows_in, axis=1, keepdims=True))
    normed = low(rows_in * lax.rsqrt(mean_sq + EPSILON) * pre_gain)
    w_in = jnp.concatenate([w_zx.reshape(D, 2 * DI), w_bc, w_dt], axis=1)
    projected = low_back(low(jnp.dot(normed, w_in, precision=HIGHEST)))
    gate_in = projected[:, :DI]
    conv_in = projected[:, DI:2 * DI + 2 * NS]
    raw_rates = projected[:, 2 * DI + 2 * NS:]
    pre_act = conv_bias + conv_weight[0] * conv_in
    for offset in range(1, KCONV):
        shifted = jnp.concatenate([jnp.zeros((offset, conv_in.shape[1]), conv_in.dtype), conv_in[:-offset]], axis=0)
        joined = jnp.concatenate([jnp.zeros((offset,), jnp.bool_), group_ids[offset:] == group_ids[:-offset]])
        pre_act = pre_act + conv_weight[offset] * shifted * joined[:, None]
    activated = silu_of(pre_act)
    inputs = low(activated[:, :DI]).reshape(GROUP, H, P_SIZE)
    b_rows = low(activated[:, DI:DI + NS])
    c_rows = low(activated[:, DI + NS:])
    state_init = jnp.zeros((H, P_SIZE, NS), conv_in.dtype)
    mixed, _, _ = state_scan(inputs, b_rows, c_rows, raw_rates, dt_bias, a_log, d_skip, group_ids, jnp.int32(-2), state_init)
    mixed = low_back(low(mixed.reshape(GROUP, DI)))
    gated_rows = mixed * silu_of(gate_in)
    row_scale = lax.rsqrt(lax.optimization_barrier(jnp.mean(gated_rows * gated_rows, axis=1, keepdims=True)) + EPSILON)
    branch = low(gated_rows * row_scale * norm_gain)
    live_rows = (group_ids >= 0).astype(rows_in.dtype)[:, None]
    return rows_in + live_rows * jnp.dot(branch, w_out, precision=HIGHEST)

def reference(residual, cotangent, seq_ids, w_zx, w_bc, w_dt, w_out, conv_weight, conv_bias, dt_bias, a_log, d_skip, norm_gain, pre_gain):
    floats = tuple((value.astype(jnp.float32) for value in (residual, w_zx, w_bc, w_dt, w_out, conv_weight, conv_bias, dt_bias, a_log, d_skip, norm_gain, pre_gain)))

    def layer_forward(residual_f, *weights):

        def one_group(group_pair):
            return group_forward(group_pair[0], group_pair[1], *weights)
        rows_out = lax.map(jax.checkpoint(one_group), (residual_f.reshape(-1, GROUP, D), seq_ids.reshape(-1, GROUP)))
        return rows_out.reshape(-1, D)
    output, pull_back = jax.vjp(layer_forward, *floats)
    grads = pull_back(cotangent.astype(jnp.float32))
    return (output, grads[0], grads[1], grads[2], grads[3], grads[4], grads[5], grads[6], grads[7], grads[8], grads[9], grads[10], grads[11])
```

```python
import jax
import jax.numpy as jnp
from jax import lax
from jax.experimental import pallas as pl
from jax.experimental.pallas import tpu as pltpu
from jax.sharding import PartitionSpec as P

BLOCK = 256


EPSILON = 1e-05
HIGHEST = lax.Precision.HIGHEST
CONTRACT_ROWS = (((0,), (0,)), ((), ()))
CONTRACT_COLS = (((1,), (1,)), ((), ()))


def silu_of(value):
    return value * jax.nn.sigmoid(value)


def silu_slope(value):
    sigmoid_val = jax.nn.sigmoid(value)
    return sigmoid_val * (1.0 + value * (1.0 - sigmoid_val))


def rounded(value):
    return lax.optimization_barrier(value.astype(jnp.bfloat16)).astype(jnp.float32)


def matmul_rows(left_mat, right_mat):
    return lax.dot_general(left_mat, right_mat, CONTRACT_ROWS, preferred_element_type=jnp.float32)


def matmul_cols(left_mat, right_mat):
    return lax.dot_general(left_mat, right_mat, CONTRACT_COLS, preferred_element_type=jnp.float32)


def put_slice(total_vec, piece_vec, first_index, axis_pos):
    return lax.dynamic_update_slice_in_dim(total_vec, piece_vec, first_index, axis_pos)


def dot_of(left_mat, right_mat, left_dim, right_dim):
    return lax.dot_general(
        left_mat,
        right_mat,
        (((left_dim,), (right_dim,)), ((), ())),
        preferred_element_type=jnp.float32,
    )


def spread(cols, expand):
    return jnp.dot(cols, expand, precision=HIGHEST, preferred_element_type=jnp.float32)


def head_decay(cum_c, cum_r, mask, head):
    gap = jnp.where(mask, cum_c[:, head : head + 1] - cum_r[head : head + 1, :], -1e30)
    return jnp.exp(gap)


def block_mask(id_c, id_r):
    size = id_c.shape[0]
    row = lax.broadcasted_iota(jnp.int32, (size, size), 0)
    col = lax.broadcasted_iota(jnp.int32, (size, size), 1)
    return (row >= col) & (id_c == id_r)


def pair_masks(size, width, heads):
    lane = lax.broadcasted_iota(jnp.int32, (size, width), 1)
    part = width // heads
    return [(lane // part) == k for k in range(heads)]


def forward_kernel(
    x_ref, b_ref, c_ref, cumc_ref, cumr_ref, dtr_ref, ec_ref, tail_ref, kept_ref, skip_ref,
    idc_ref, idr_ref, expand_ref, y_ref, h_ref, state,
):
    heads = cumc_ref.shape[1]
    size, inner = x_ref.shape
    per = 128 * heads // inner

    @pl.when(pl.program_id(0) == 0)
    def _():
        state[...] = jnp.zeros_like(state)

    expand = expand_ref[...]
    x, b, c = x_ref[...], b_ref[...], c_ref[...]
    h_low = state[...].astype(jnp.bfloat16)
    h_ref[0] = h_low
    x_f = x.astype(jnp.float32)
    y_all = dot_of(c, h_low, 1, 0) * spread(ec_ref[...], expand) + skip_ref[...] * x_f
    scores = dot_of(c, b, 1, 1)
    mask = block_mask(idc_ref[...], idr_ref[...])
    cum_c, cum_r, dt_r = cumc_ref[...], cumr_ref[...], dtr_ref[...]
    sides = pair_masks(size, 128, per)
    for pair in range(heads // per):
        lanes = slice(128 * pair, 128 * pair + 128)
        x_pair = x[:, lanes]
        acc = y_all[:, lanes]
        for k in range(per):
            head = pair * per + k
            mix = scores * head_decay(cum_c, cum_r, mask, head) * dt_r[head : head + 1, :]
            part = jnp.where(sides[k], x_pair, jnp.zeros_like(x_pair))
            acc = acc + dot_of(mix.astype(jnp.bfloat16), part, 1, 0)
        y_ref[:, lanes] = acc.astype(y_ref.dtype)
    tail = spread(tail_ref[...], expand)
    state[...] = state[...] * kept_ref[0] + dot_of(b, (x_f * tail).astype(jnp.bfloat16), 0, 0)


def backward_kernel(
    x_ref, dy_ref, b_ref, c_ref, cumc_ref, cumr_ref, dtr_ref, ec_ref, tail_ref, rate_ref,
    kept_ref, skip_ref, idc_ref, idr_ref, expand_ref, h_ref,
    dx_ref, db_ref, dc_ref, row_ref, late_ref, col_ref, keep_ref, dskip_ref, grad,
):
    heads = cumc_ref.shape[1]
    size, inner = x_ref.shape
    per = 128 * heads // inner

    @pl.when(pl.program_id(0) == 0)
    def _():
        grad[...] = jnp.zeros_like(grad)

    expand = expand_ref[...]
    x, dy, b, c, h_low = x_ref[...], dy_ref[...], b_ref[...], c_ref[...], h_ref[0]
    x_f, dy_f = x.astype(jnp.float32), dy.astype(jnp.float32)
    g_now = grad[...]
    g_low = g_now.astype(jnp.bfloat16)
    early = spread(ec_ref[...], expand)
    tail = spread(tail_ref[...], expand)
    dy_early = dy_f * early
    dy_early_low = dy_early.astype(jnp.bfloat16)
    from_state = dot_of(c, h_low, 1, 0)
    to_state = dot_of(b, g_low, 1, 0)

    def by_head(value):
        return lax.dot_general(
            value, expand, CONTRACT_COLS, precision=HIGHEST, preferred_element_type=jnp.float32
        )

    late_ref[...] = by_head(x_f * to_state) * rate_ref[...]
    row_sums = by_head(dy_early * from_state)
    keep_ref[0] = jnp.sum(h_low.astype(jnp.float32) * g_now, axis=0, keepdims=True) * kept_ref[0]
    dskip_ref[0] = jnp.sum(x_f * dy_f, axis=0, keepdims=True)
    grad[...] = g_now * kept_ref[0] + dot_of(c, dy_early_low, 0, 0)
    dx_all = skip_ref[...] * dy_f + tail * to_state
    scores = dot_of(c, b, 1, 1)
    mask = block_mask(idc_ref[...], idr_ref[...])
    cum_c, cum_r, dt_r = cumc_ref[...], cumr_ref[...], dtr_ref[...]
    sides = pair_masks(size, 128, per)
    head_lane = lax.broadcasted_iota(jnp.int32, (size, heads), 1)
    d_scores = jnp.zeros((size, size), jnp.float32)
    for pair in range(heads // per):
        lanes = slice(128 * pair, 128 * pair + 128)
        x_pair, dy_pair = x[:, lanes], dy[:, lanes]
        acc = dx_all[:, lanes]
        for k in range(per):
            head = pair * per + k
            decay = head_decay(cum_c, cum_r, mask, head)
            dt_row = dt_r[head : head + 1, :]
            dy_part = jnp.where(sides[k], dy_pair, jnp.zeros_like(dy_pair))
            d_mix = dot_of(dy_part, x_pair, 1, 1) * decay
            d_scores = d_scores + d_mix * dt_row
            core = d_mix * scores
            col_ref[head : head + 1, :] = jnp.sum(core, axis=0, keepdims=True)
            row_sum = jnp.sum(core * dt_row, axis=1, keepdims=True)
            row_sums = row_sums + jnp.where(head_lane == head, row_sum, 0.0)
            mix = (scores * decay * dt_row).astype(jnp.bfloat16)
            acc = acc + dot_of(mix, dy_part, 0, 0)
        dx_ref[:, lanes] = acc
    row_ref[...] = row_sums
    d_low = d_scores.astype(jnp.bfloat16)
    dc_ref[...] = dot_of(d_low, b, 1, 0) + dot_of(dy_early_low, h_low, 1, 1)
    db_ref[...] = dot_of(d_low, c, 0, 0) + dot_of((x_f * tail).astype(jnp.bfloat16), g_low, 1, 1)


def scan_terms(raw_rates, bias_vec, log_rates, skip_gain, ids, inner):
    rows, heads = raw_rates.shape
    count = rows // BLOCK
    step = jax.nn.softplus(raw_rates + bias_vec)
    rate = -jnp.exp(log_rates)
    decay = rate * step
    lower = (jnp.arange(BLOCK)[:, None] >= jnp.arange(BLOCK)[None, :]).astype(jnp.float32)
    cum = jnp.einsum(
        "ij,bjh->bih", lower, decay.reshape(count, BLOCK, heads), precision=HIGHEST
    )
    blocks = ids.reshape(count, BLOCK)
    before = jnp.concatenate([jnp.full((1,), -2, ids.dtype), blocks[:-1, -1]])
    joins = (blocks == before[:, None])[:, :, None]
    stays = (blocks == blocks[:, -1:])[:, :, None]
    early = jnp.where(joins, jnp.exp(cum), 0.0)
    rest = jnp.where(stays, jnp.exp(cum[:, -1:] - cum), 0.0)
    tail = rest * step.reshape(count, BLOCK, heads)
    part = inner // heads
    kept = jnp.repeat(early[:, -1:], part, axis=2)
    expand = jnp.repeat(jnp.eye(heads, dtype=jnp.float32), part, axis=1)

    def flat(value):
        return value.reshape(rows, heads)

    return dict(
        step=step, decay=decay, rate=rate, lower=lower, count=count, kept=kept, expand=expand,
        cum=flat(cum), cum_r=flat(cum).T, step_r=step.T, early=flat(early), rest=flat(rest),
        tail=flat(tail), skip=jnp.repeat(skip_gain, part)[None, :],
        ids_c=ids[:, None], ids_r=ids[None, :],
    )


def scan_forward(x, b, c, t):
    rows, inner = x.shape
    width, heads = b.shape[1], t["cum"].shape[1]

    def tall(cols):
        return pl.BlockSpec((BLOCK, cols), lambda i: (i, 0))

    def wide(rows_):
        return pl.BlockSpec((rows_, BLOCK), lambda i: (0, i))

    def whole(shape):
        return pl.BlockSpec(shape, lambda i: (0, 0))

    per_block = pl.BlockSpec((1, 1, inner), lambda i: (i, 0, 0))
    return pl.pallas_call(
        forward_kernel,
        grid=(t["count"],),
        in_specs=[
            tall(inner), tall(width), tall(width), tall(heads), wide(heads), wide(heads),
            tall(heads), tall(heads), per_block, whole((1, inner)), tall(1), wide(1),
            whole((heads, inner)),
        ],
        out_specs=[tall(inner), pl.BlockSpec((1, width, inner), lambda i: (i, 0, 0))],
        out_shape=[
            jax.ShapeDtypeStruct((rows, inner), jnp.bfloat16),
            jax.ShapeDtypeStruct((t["count"], width, inner), jnp.bfloat16),
        ],
        scratch_shapes=[pltpu.VMEM((width, inner), jnp.float32)],
        compiler_params=pltpu.CompilerParams(vmem_limit_bytes=40 * 2**20),
        cost_estimate=pl.CostEstimate(
            flops=4 * 10**9, bytes_accessed=8 * 2**20, transcendentals=4 * 2**20
        ),
        name="scan_forward",
    )(
        x, b, c, t["cum"], t["cum_r"], t["step_r"], t["early"], t["tail"], t["kept"], t["skip"],
        t["ids_c"], t["ids_r"], t["expand"],
    )


def scan_backward(x, dy, b, c, states, t):
    rows, inner = x.shape
    width, heads = b.shape[1], t["cum"].shape[1]
    last = t["count"] - 1

    def tall(cols):
        return pl.BlockSpec((BLOCK, cols), lambda i: (last - i, 0))

    def wide(rows_):
        return pl.BlockSpec((rows_, BLOCK), lambda i: (0, last - i))

    def whole(shape):
        return pl.BlockSpec(shape, lambda i: (0, 0))

    per_block = pl.BlockSpec((1, 1, inner), lambda i: (last - i, 0, 0))
    f32 = jnp.float32
    dx, db, dc, row, late, col, keep, dskip = pl.pallas_call(
        backward_kernel,
        grid=(t["count"],),
        in_specs=[
            tall(inner), tall(inner), tall(width), tall(width), tall(heads), wide(heads),
            wide(heads), tall(heads), tall(heads), tall(heads), per_block, whole((1, inner)),
            tall(1), wide(1), whole((heads, inner)),
            pl.BlockSpec((1, width, inner), lambda i: (last - i, 0, 0)),
        ],
        out_specs=[
            tall(inner), tall(width), tall(width), tall(heads), tall(heads), wide(heads),
            per_block, per_block,
        ],
        out_shape=[
            jax.ShapeDtypeStruct((rows, inner), f32),
            jax.ShapeDtypeStruct((rows, width), f32),
            jax.ShapeDtypeStruct((rows, width), f32),
            jax.ShapeDtypeStruct((rows, heads), f32),
            jax.ShapeDtypeStruct((rows, heads), f32),
            jax.ShapeDtypeStruct((heads, rows), f32),
            jax.ShapeDtypeStruct((t["count"], 1, inner), f32),
            jax.ShapeDtypeStruct((t["count"], 1, inner), f32),
        ],
        scratch_shapes=[pltpu.VMEM((width, inner), f32)],
        compiler_params=pltpu.CompilerParams(vmem_limit_bytes=40 * 2**20),
        cost_estimate=pl.CostEstimate(
            flops=10 * 10**9, bytes_accessed=16 * 2**20, transcendentals=4 * 2**20
        ),
        name="scan_backward",
    )(
        x, dy, b, c, t["cum"], t["cum_r"], t["step_r"], t["early"], t["tail"], t["rest"],
        t["kept"], t["skip"], t["ids_c"], t["ids_r"], t["expand"], states,
    )
    count = t["count"]
    direct = col.T + late
    after = row - direct * t["step"]
    ends = jnp.sum((late * t["step"]).reshape(count, BLOCK, heads), axis=1)
    ends = ends + jnp.sum(keep.reshape(count, heads, -1), axis=2)
    d_decay = jnp.einsum(
        "ij,bih->bjh", t["lower"], after.reshape(count, BLOCK, heads), precision=HIGHEST
    )
    d_decay = (d_decay + ends[:, None, :]).reshape(rows, heads)
    d_step = direct + t["rate"] * d_decay
    d_logs = jnp.sum(d_decay * t["decay"], axis=0)
    d_skip = jnp.sum(dskip.reshape(count, heads, -1), axis=(0, 2))
    return dx, db, dc, d_step, d_logs, d_skip


def conv_apply(conv_in, weight, bias_vec, row_ids, rim_rows, rim_ids):
    row_count = conv_in.shape[0]
    margin = rim_rows.shape[0]
    extended = jnp.concatenate([rim_rows, conv_in], axis=0)
    extended_ids = jnp.concatenate([rim_ids, row_ids])
    pre_act = bias_vec + weight[0] * conv_in
    for offset in range(1, weight.shape[0]):
        shifted = extended[margin - offset : margin - offset + row_count]
        joined = extended_ids[margin - offset : margin - offset + row_count] == row_ids
        pre_act = pre_act + weight[offset] * shifted * joined[:, None]
    return silu_of(pre_act)


def local(
    residual,
    cotangent,
    seq_ids,
    w_zx,
    w_bc,
    w_dt,
    w_out,
    conv_weight,
    conv_bias,
    dt_bias,
    a_log,
    d_skip,
    norm_gain,
    pre_gain,
):
    tensor_index = lax.axis_index("tensor")
    own_rows = residual.shape[0]
    group_rows = seq_ids.shape[0]
    model_width = residual.shape[1]
    state_width = w_bc.shape[1] // 2
    heads_all = dt_bias.shape[0]
    inner_all = norm_gain.shape[0]
    head_dim = inner_all // heads_all
    margin = conv_weight.shape[0] - 1
    channels_all = conv_weight.shape[1]
    residual_f = residual.astype(jnp.float32)
    inv_rms = lax.rsqrt(jnp.mean(residual_f * residual_f, axis=1, keepdims=True) + EPSILON)
    normed = (residual_f * inv_rms * pre_gain).astype(jnp.bfloat16)
    dt_cols, zx_cols = w_dt.shape[1], w_zx.shape[1] * w_zx.shape[2]
    w_part = jnp.concatenate([w_zx.reshape(w_zx.shape[0], zx_cols), w_bc, w_dt], axis=1)
    w_local = lax.all_gather(w_part, "dp", axis=0, tiled=True)
    out_wt = lax.all_gather(w_out.T, "dp", axis=0, tiled=True)
    bc_w = w_local[:, zx_cols : zx_cols + 2 * state_width]
    own_ids = lax.dynamic_slice_in_dim(seq_ids, tensor_index * own_rows, own_rows)
    live_rows = (own_ids >= 0).astype(jnp.float32)[:, None]
    grad_cot = cotangent * live_rows.astype(jnp.bfloat16)
    heads_here = dt_cols
    inner_here = heads_here * head_dim
    col_start = tensor_index * inner_here
    head_start = tensor_index * heads_here
    rows_normed = lax.all_gather(normed, "tensor", axis=0, tiled=True)
    projected = jnp.dot(rows_normed, w_local, preferred_element_type=jnp.float32).astype(
        jnp.bfloat16
    )
    gate_in = projected[:, :inner_here].astype(jnp.float32)
    conv_in = projected[:, inner_here : 2 * inner_here + 2 * state_width]
    raw_rates = projected[:, 2 * inner_here + 2 * state_width :]
    conv_w_here = jnp.concatenate(
        [
            lax.dynamic_slice_in_dim(conv_weight, col_start, inner_here, 1),
            conv_weight[:, inner_all:],
        ],
        axis=1,
    )
    conv_b_here = jnp.concatenate(
        [lax.dynamic_slice_in_dim(conv_bias, col_start, inner_here), conv_bias[inner_all:]]
    )
    dt_b_here = lax.dynamic_slice_in_dim(dt_bias, head_start, heads_here)
    logs_here = lax.dynamic_slice_in_dim(a_log, head_start, heads_here)
    skip_here = lax.dynamic_slice_in_dim(d_skip, head_start, heads_here)
    gain_here = lax.dynamic_slice_in_dim(norm_gain, col_start, inner_here)
    rim_rows = jnp.zeros((margin, conv_in.shape[1]), jnp.float32)
    rim_ids = jnp.full((margin,), -2, jnp.int32)

    def conv_local(values, weight, bias_vec):
        return conv_apply(values, weight, bias_vec, seq_ids, rim_rows, rim_ids)

    activated, conv_pull = jax.vjp(
        conv_local, conv_in.astype(jnp.float32), conv_w_here, conv_b_here
    )
    activated = lax.optimization_barrier(activated.astype(jnp.bfloat16))
    inputs = activated[:, :inner_here]
    b_rows = activated[:, inner_here : inner_here + state_width]
    c_rows = activated[:, inner_here + state_width :]
    raw_f = raw_rates.astype(jnp.float32)
    terms = scan_terms(raw_f, dt_b_here, logs_here, skip_here, seq_ids, inner_here)
    mixed, states = scan_forward(inputs, b_rows, c_rows, terms)
    mixed_f = mixed.astype(jnp.float32)
    gate_act = silu_of(gate_in)
    gated_rows = mixed_f * gate_act
    sum_sq = lax.psum(jnp.sum(gated_rows * gated_rows, axis=1), "tensor")
    row_scale = lax.rsqrt(sum_sq / inner_all + EPSILON)[:, None]
    branch = (gated_rows * row_scale * gain_here).astype(jnp.bfloat16)
    mix_rows = lax.psum_scatter(
        matmul_cols(branch, out_wt).astype(jnp.bfloat16),
        "tensor",
        scatter_dimension=0,
        tiled=True,
    ).astype(jnp.float32)
    output = residual_f + live_rows * mix_rows
    cot_rows = lax.all_gather(grad_cot, "tensor", axis=0, tiled=True)
    grad_out_w = matmul_rows(cot_rows, branch).astype(jnp.bfloat16)
    grad_out_w = lax.psum_scatter(grad_out_w, "dp", scatter_dimension=0, tiled=True)
    grad_branch = jnp.dot(cot_rows, out_wt, preferred_element_type=jnp.float32)
    weighted = grad_branch * gain_here
    dots_total = lax.psum(jnp.sum(weighted * gated_rows, axis=1), "tensor")
    grad_gated = (
        row_scale * weighted - gated_rows * row_scale**3 * (dots_total / inner_all)[:, None]
    )
    gain_local = jnp.sum(grad_branch * gated_rows * row_scale, axis=0)
    grad_mixed = (grad_gated * gate_act).astype(jnp.bfloat16)
    grad_gate = (grad_gated * mixed_f * silu_slope(gate_in)).astype(jnp.bfloat16)
    grad_inputs, grad_b, grad_c, grad_step, grad_logs, grad_skip = scan_backward(
        inputs, grad_mixed, b_rows, c_rows, states, terms
    )
    grad_raw = grad_step * jax.nn.sigmoid(raw_f + dt_b_here)
    grad_dt_b = jnp.sum(grad_raw, axis=0)
    grad_conv_in, grad_conv_w, grad_conv_b = conv_pull(
        jnp.concatenate([grad_inputs, grad_b, grad_c], axis=1)
    )
    grad_bc = lax.psum(grad_conv_in[:, inner_here:].astype(jnp.bfloat16), "tensor")
    own_index = lax.broadcasted_iota(jnp.int32, (group_rows, 1), 0) // own_rows
    own_bc = jnp.where(own_index == tensor_index, grad_bc, jnp.zeros_like(grad_bc))
    grad_gate_in = jnp.concatenate([grad_gate, grad_conv_in[:, :inner_here].astype(jnp.bfloat16)], axis=1)
    grad_raw_low = grad_raw.astype(jnp.bfloat16)
    grad_all = jnp.concatenate([grad_gate_in, grad_bc, grad_raw_low], axis=1)
    grad_in_w = matmul_rows(rows_normed, grad_all).astype(jnp.bfloat16)
    grad_in_w = lax.psum_scatter(grad_in_w, "dp", scatter_dimension=0, tiled=True)
    grad_mine = jnp.concatenate([grad_gate_in, own_bc, grad_raw_low], axis=1)
    grad_normed = lax.psum_scatter(
        matmul_cols(grad_mine, w_local).astype(jnp.bfloat16),
        "tensor",
        scatter_dimension=0,
        tiled=True,
    ).astype(jnp.float32)
    conv_w_full = jnp.zeros((margin + 1, channels_all), jnp.float32)
    conv_w_full = put_slice(conv_w_full, grad_conv_w[:, :inner_here], col_start, 1)
    conv_w_full = put_slice(conv_w_full, grad_conv_w[:, inner_here:], inner_all, 1)
    conv_b_full = jnp.zeros((channels_all,), jnp.float32)
    conv_b_full = put_slice(conv_b_full, grad_conv_b[:inner_here], col_start, 0)
    conv_b_full = put_slice(conv_b_full, grad_conv_b[inner_here:], inner_all, 0)
    dt_b_full = put_slice(jnp.zeros((heads_all,), jnp.float32), grad_dt_b, head_start, 0)
    logs_full = put_slice(jnp.zeros((heads_all,), jnp.float32), grad_logs, head_start, 0)
    skip_full = put_slice(jnp.zeros((heads_all,), jnp.float32), grad_skip, head_start, 0)
    gain_full = put_slice(jnp.zeros((inner_all,), jnp.float32), gain_local, col_start, 0)
    grad_pre = jnp.sum(grad_normed * residual_f * inv_rms, axis=0)
    grad_residual = (
        cotangent.astype(jnp.float32)
        + inv_rms * pre_gain * grad_normed
        - residual_f
        * inv_rms**3
        * jnp.mean(grad_normed * pre_gain * residual_f, axis=1, keepdims=True)
    )
    grad_in_w = grad_in_w.astype(jnp.float32)
    grad_zx_w = grad_in_w[:, :zx_cols].reshape(w_zx.shape)
    grad_bc_w = grad_in_w[:, zx_cols : zx_cols + 2 * state_width]
    grad_dt_w = grad_in_w[:, zx_cols + 2 * state_width :]
    grad_out_w = grad_out_w.astype(jnp.float32).T
    small = [conv_w_full, conv_b_full, dt_b_full, logs_full, skip_full, gain_full, grad_pre]
    packed = lax.psum(jnp.concatenate([part.reshape(-1) for part in small]), ("dp", "tensor"))
    small_sums, first = [], 0
    for part in small:
        small_sums.append(packed[first : first + part.size].reshape(part.shape))
        first += part.size
    return (
        output,
        grad_residual,
        grad_zx_w,
        grad_bc_w,
        grad_dt_w,
        grad_out_w,
        small_sums[0],
        small_sums[1],
        small_sums[2],
        small_sums[3],
        small_sums[4],
        small_sums[5],
        small_sums[6],
    )


def solution(mesh):
    placed = (
        P(("dp", "tensor"), None),
        P(("dp", "tensor"), None),
        P("dp"),
        P("dp", None, "tensor"),
        P("dp", None),
        P("dp", "tensor"),
        P("tensor", "dp"),
        P(),
        P(),
        P(),
        P(),
        P(),
        P(),
        P(),
    )
    return jax.shard_map(
        local,
        mesh=mesh,
        in_specs=placed,
        out_specs=(
            P(("dp", "tensor"), None),
            P(("dp", "tensor"), None),
            P("dp", None, "tensor"),
            P("dp", None),
            P("dp", "tensor"),
            P("tensor", "dp"),
            P(),
            P(),
            P(),
            P(),
            P(),
            P(),
            P(),
        ),
        check_vma=False,
    )
```

```python
import jax
import jax.numpy as jnp
from jax import lax
from jax.experimental import pallas as pl
from jax.experimental.pallas import tpu as pltpu
from jax.sharding import PartitionSpec as P

BLOCK = 256


EPSILON = 1e-05
HIGHEST = lax.Precision.HIGHEST
CONTRACT_ROWS = (((0,), (0,)), ((), ()))
CONTRACT_COLS = (((1,), (1,)), ((), ()))


def silu_of(value):
    return value * jax.nn.sigmoid(value)


def silu_slope(value):
    sigmoid_val = jax.nn.sigmoid(value)
    return sigmoid_val * (1.0 + value * (1.0 - sigmoid_val))


def rounded(value):
    return lax.optimization_barrier(value.astype(jnp.bfloat16)).astype(jnp.float32)


def matmul_rows(left_mat, right_mat):
    return lax.dot_general(left_mat, right_mat, CONTRACT_ROWS, preferred_element_type=jnp.float32)


def matmul_cols(left_mat, right_mat):
    return lax.dot_general(left_mat, right_mat, CONTRACT_COLS, preferred_element_type=jnp.float32)


def put_slice(total_vec, piece_vec, first_index, axis_pos):
    return lax.dynamic_update_slice_in_dim(total_vec, piece_vec, first_index, axis_pos)


def dot_of(left_mat, right_mat, left_dim, right_dim):
    return lax.dot_general(
        left_mat,
        right_mat,
        (((left_dim,), (right_dim,)), ((), ())),
        preferred_element_type=jnp.float32,
    )


def spread(cols, expand):
    return jnp.dot(cols, expand, precision=HIGHEST, preferred_element_type=jnp.float32)


def head_decay(cum_c, cum_r, mask, head):
    gap = jnp.where(mask, cum_c[:, head : head + 1] - cum_r[head : head + 1, :], -1e30)
    return jnp.exp(gap)


def block_mask(id_c, id_r):
    size = id_c.shape[0]
    row = lax.broadcasted_iota(jnp.int32, (size, size), 0)
    col = lax.broadcasted_iota(jnp.int32, (size, size), 1)
    return (row >= col) & (id_c == id_r)


def pair_masks(size, width, heads):
    lane = lax.broadcasted_iota(jnp.int32, (size, width), 1)
    part = width // heads
    return [(lane // part) == k for k in range(heads)]


def forward_kernel(
    u_ref, taps_ref, bias_ref, joins_ref, cumc_ref, cumr_ref, dtr_ref, ec_ref, tail_ref, kept_ref,
    skip_ref, idc_ref, idr_ref, expand_ref, y_ref, h_ref, act_ref, state, ext,
):
    heads = cumc_ref.shape[1]
    size, inner = y_ref.shape
    width = (u_ref.shape[1] - inner) // 2
    per = 128 * heads // inner

    @pl.when(pl.program_id(0) == 0)
    def _():
        state[...] = jnp.zeros_like(state)
        ext[size : size + 8, :] = jnp.zeros((8, ext.shape[1]), jnp.float32)

    expand = expand_ref[...]
    joins = joins_ref[...]
    ext[0:8, :] = ext[size : size + 8, :]
    ext[8 : size + 8, :] = u_ref[...].astype(jnp.float32)
    for first in range(0, u_ref.shape[1], 128):
        lanes = slice(first, first + 128)
        pre = bias_ref[:, lanes] + taps_ref[0:1, lanes] * ext[8 : size + 8, lanes]
        for k in range(1, taps_ref.shape[0]):
            shifted = ext[8 - k : size + 8 - k, lanes] * joins[:, k - 1 : k]
            pre = pre + taps_ref[k : k + 1, lanes] * shifted
        act_ref[:, lanes] = silu_of(pre).astype(act_ref.dtype)
    x = act_ref[:, :inner]
    b = act_ref[:, inner : inner + width]
    c = act_ref[:, inner + width :]
    h_low = state[...].astype(jnp.bfloat16)
    h_ref[0] = h_low
    x_f = x.astype(jnp.float32)
    y_all = dot_of(c, h_low, 1, 0) * spread(ec_ref[...], expand) + skip_ref[...] * x_f
    scores = dot_of(c, b, 1, 1)
    mask = block_mask(idc_ref[...], idr_ref[...])
    cum_c, cum_r, dt_r = cumc_ref[...], cumr_ref[...], dtr_ref[...]
    sides = pair_masks(size, 128, per)
    for pair in range(heads // per):
        lanes = slice(128 * pair, 128 * pair + 128)
        x_pair = x[:, lanes]
        acc = y_all[:, lanes]
        for k in range(per):
            head = pair * per + k
            mix = scores * head_decay(cum_c, cum_r, mask, head) * dt_r[head : head + 1, :]
            part = jnp.where(sides[k], x_pair, jnp.zeros_like(x_pair))
            acc = acc + dot_of(mix.astype(jnp.bfloat16), part, 1, 0)
        y_ref[:, lanes] = acc.astype(y_ref.dtype)
    tail = spread(tail_ref[...], expand)
    state[...] = state[...] * kept_ref[0] + dot_of(b, (x_f * tail).astype(jnp.bfloat16), 0, 0)


def backward_kernel(
    act_ref, u_ref, past_ref, dy_ref, taps_ref, bias_ref, joins_ref, nexts_ref,
    cumc_ref, cumr_ref, dtr_ref, ec_ref, tail_ref, rate_ref,
    kept_ref, skip_ref, idc_ref, idr_ref, expand_ref, h_ref,
    du_ref, conv_ref, row_ref, late_ref, col_ref, keep_ref, dskip_ref, grad, ext, past,
):
    heads = cumc_ref.shape[1]
    size, inner = dy_ref.shape
    width = (u_ref.shape[1] - inner) // 2
    tap_count = taps_ref.shape[0]
    per = 128 * heads // inner

    @pl.when(pl.program_id(0) == 0)
    def _():
        grad[...] = jnp.zeros_like(grad)
        conv_ref[...] = jnp.zeros_like(conv_ref)
        ext[0:8, :] = jnp.zeros((8, ext.shape[1]), jnp.float32)

    ext[size : size + 8, :] = ext[0:8, :]
    past[0:16, :] = past_ref[...].astype(jnp.float32)
    past[16 : size + 16, :] = u_ref[...].astype(jnp.float32)
    expand = expand_ref[...]
    dy, h_low = dy_ref[...], h_ref[0]
    x = act_ref[:, :inner]
    b = act_ref[:, inner : inner + width]
    c = act_ref[:, inner + width :]
    x_f, dy_f = x.astype(jnp.float32), dy.astype(jnp.float32)
    g_now = grad[...]
    g_low = g_now.astype(jnp.bfloat16)
    early = spread(ec_ref[...], expand)
    tail = spread(tail_ref[...], expand)
    dy_early = dy_f * early
    dy_early_low = dy_early.astype(jnp.bfloat16)
    from_state = dot_of(c, h_low, 1, 0)
    to_state = dot_of(b, g_low, 1, 0)

    def by_head(value):
        return lax.dot_general(
            value, expand, CONTRACT_COLS, precision=HIGHEST, preferred_element_type=jnp.float32
        )

    late_ref[...] = by_head(x_f * to_state) * rate_ref[...]
    row_sums = by_head(dy_early * from_state)
    keep_ref[0] = jnp.sum(h_low.astype(jnp.float32) * g_now, axis=0, keepdims=True) * kept_ref[0]
    dskip_ref[0] = jnp.sum(x_f * dy_f, axis=0, keepdims=True)
    grad[...] = g_now * kept_ref[0] + dot_of(c, dy_early_low, 0, 0)
    dx_all = skip_ref[...] * dy_f + tail * to_state
    scores = dot_of(c, b, 1, 1)
    mask = block_mask(idc_ref[...], idr_ref[...])
    cum_c, cum_r, dt_r = cumc_ref[...], cumr_ref[...], dtr_ref[...]
    sides = pair_masks(size, 128, per)
    head_lane = lax.broadcasted_iota(jnp.int32, (size, heads), 1)
    d_scores = jnp.zeros((size, size), jnp.float32)
    for pair in range(heads // per):
        lanes = slice(128 * pair, 128 * pair + 128)
        x_pair, dy_pair = x[:, lanes], dy[:, lanes]
        acc = dx_all[:, lanes]
        for k in range(per):
            head = pair * per + k
            decay = head_decay(cum_c, cum_r, mask, head)
            dt_row = dt_r[head : head + 1, :]
            dy_part = jnp.where(sides[k], dy_pair, jnp.zeros_like(dy_pair))
            d_mix = dot_of(dy_part, x_pair, 1, 1) * decay
            d_scores = d_scores + d_mix * dt_row
            core = d_mix * scores
            col_ref[head : head + 1, :] = jnp.sum(core, axis=0, keepdims=True)
            row_sum = jnp.sum(core * dt_row, axis=1, keepdims=True)
            row_sums = row_sums + jnp.where(head_lane == head, row_sum, 0.0)
            mix = (scores * decay * dt_row).astype(jnp.bfloat16)
            acc = acc + dot_of(mix, dy_part, 0, 0)
        ext[0:size, lanes] = acc
    row_ref[...] = row_sums
    d_low = d_scores.astype(jnp.bfloat16)
    x_tail = (x_f * tail).astype(jnp.bfloat16)
    ext[0:size, inner : inner + width] = dot_of(d_low, c, 0, 0) + dot_of(x_tail, g_low, 1, 1)
    ext[0:size, inner + width :] = dot_of(d_low, b, 1, 0) + dot_of(dy_early_low, h_low, 1, 1)
    joins, nexts = joins_ref[...], nexts_ref[...]
    for first in range(0, u_ref.shape[1], 128):
        lanes = slice(first, first + 128)
        moved = [past[16 : size + 16, lanes]]
        for k in range(1, tap_count):
            moved.append(past[16 - k : size + 16 - k, lanes] * joins[:, k - 1 : k])
        pre = bias_ref[:, lanes]
        for k in range(tap_count):
            pre = pre + taps_ref[k : k + 1, lanes] * moved[k]
        d_pre = ext[0:size, lanes] * silu_slope(pre)
        ext[0:size, lanes] = d_pre
        for k in range(tap_count):
            conv_ref[k : k + 1, lanes] += jnp.sum(d_pre * moved[k], axis=0, keepdims=True)
        conv_ref[tap_count : tap_count + 1, lanes] += jnp.sum(d_pre, axis=0, keepdims=True)
        du = taps_ref[0:1, lanes] * d_pre
        for k in range(1, tap_count):
            later = ext[k : size + k, lanes] * nexts[:, k - 1 : k]
            du = du + taps_ref[k : k + 1, lanes] * later
        du_ref[:, lanes] = du.astype(du_ref.dtype)


def scan_terms(raw_rates, bias_vec, log_rates, skip_gain, ids, inner, taps, conv_bias):
    rows, heads = raw_rates.shape
    count = rows // BLOCK
    step = jax.nn.softplus(raw_rates + bias_vec)
    rate = -jnp.exp(log_rates)
    decay = rate * step
    lower = (jnp.arange(BLOCK)[:, None] >= jnp.arange(BLOCK)[None, :]).astype(jnp.float32)
    cum = jnp.einsum(
        "ij,bjh->bih", lower, decay.reshape(count, BLOCK, heads), precision=HIGHEST
    )
    blocks = ids.reshape(count, BLOCK)
    before = jnp.concatenate([jnp.full((1,), -2, ids.dtype), blocks[:-1, -1]])
    joins = (blocks == before[:, None])[:, :, None]
    stays = (blocks == blocks[:, -1:])[:, :, None]
    early = jnp.where(joins, jnp.exp(cum), 0.0)
    rest = jnp.where(stays, jnp.exp(cum[:, -1:] - cum), 0.0)
    tail = rest * step.reshape(count, BLOCK, heads)
    part = inner // heads
    kept = jnp.repeat(early[:, -1:], part, axis=2)
    expand = jnp.repeat(jnp.eye(heads, dtype=jnp.float32), part, axis=1)

    joins, nexts = [], []
    for k in range(1, taps.shape[0]):
        same = (ids[k:] == ids[:-k]).astype(jnp.float32)
        joins.append(jnp.pad(same, (k, 0)))
        nexts.append(jnp.pad(same, (0, k)))

    def flat(value):
        return value.reshape(rows, heads)

    return dict(
        step=step, decay=decay, rate=rate, lower=lower, count=count, kept=kept, expand=expand,
        cum=flat(cum), cum_r=flat(cum).T, step_r=step.T, early=flat(early), rest=flat(rest),
        tail=flat(tail), skip=jnp.repeat(skip_gain, part)[None, :],
        ids_c=ids[:, None], ids_r=ids[None, :], joins=jnp.stack(joins, axis=1),
        nexts=jnp.stack(nexts, axis=1), taps=taps, conv_bias=conv_bias[None, :],
    )


def scan_forward(u, t):
    rows, heads = t["cum"].shape
    inner = t["expand"].shape[1]
    channels = t["taps"].shape[1]
    width = (channels - inner) // 2
    shifts = t["joins"].shape[1]

    def tall(cols):
        return pl.BlockSpec((BLOCK, cols), lambda i: (i, 0))

    def wide(rows_):
        return pl.BlockSpec((rows_, BLOCK), lambda i: (0, i))

    def whole(shape):
        return pl.BlockSpec(shape, lambda i: (0, 0))

    per_block = pl.BlockSpec((1, 1, inner), lambda i: (i, 0, 0))
    return pl.pallas_call(
        forward_kernel,
        grid=(t["count"],),
        in_specs=[
            tall(channels), whole(t["taps"].shape), whole((1, channels)), tall(shifts),
            tall(heads), wide(heads), wide(heads), tall(heads), tall(heads), per_block,
            whole((1, inner)), tall(1), wide(1), whole((heads, inner)),
        ],
        out_specs=[
            tall(inner),
            pl.BlockSpec((1, width, inner), lambda i: (i, 0, 0)),
            tall(channels),
        ],
        out_shape=[
            jax.ShapeDtypeStruct((rows, inner), jnp.bfloat16),
            jax.ShapeDtypeStruct((t["count"], width, inner), jnp.bfloat16),
            jax.ShapeDtypeStruct((rows, channels), jnp.bfloat16),
        ],
        scratch_shapes=[
            pltpu.VMEM((width, inner), jnp.float32),
            pltpu.VMEM((BLOCK + 8, channels), jnp.float32),
        ],
        compiler_params=pltpu.CompilerParams(vmem_limit_bytes=40 * 2**20),
        cost_estimate=pl.CostEstimate(
            flops=4 * 10**9, bytes_accessed=8 * 2**20, transcendentals=4 * 2**20
        ),
        name="scan_forward",
    )(
        u, t["taps"], t["conv_bias"], t["joins"], t["cum"], t["cum_r"], t["step_r"], t["early"],
        t["tail"], t["kept"], t["skip"], t["ids_c"], t["ids_r"], t["expand"],
    )


def scan_backward(act, u, dy, states, t):
    rows, heads = t["cum"].shape
    inner = t["expand"].shape[1]
    channels = t["taps"].shape[1]
    width = (channels - inner) // 2
    shifts = t["joins"].shape[1]
    last = t["count"] - 1

    def tall(cols):
        return pl.BlockSpec((BLOCK, cols), lambda i: (last - i, 0))

    def wide(rows_):
        return pl.BlockSpec((rows_, BLOCK), lambda i: (0, last - i))

    def whole(shape):
        return pl.BlockSpec(shape, lambda i: (0, 0))

    per_block = pl.BlockSpec((1, 1, inner), lambda i: (last - i, 0, 0))
    f32 = jnp.float32
    du, conv, row, late, col, keep, dskip = pl.pallas_call(
        backward_kernel,
        grid=(t["count"],),
        in_specs=[
            tall(channels), tall(channels),
            pl.BlockSpec(
                (16, channels), lambda i: (jnp.maximum((last - i) * (BLOCK // 16) - 1, 0), 0)
            ),
            tall(inner), whole(t["taps"].shape), whole((1, channels)), tall(shifts), tall(shifts),
            tall(heads), wide(heads),
            wide(heads), tall(heads), tall(heads), tall(heads), per_block, whole((1, inner)),
            tall(1), wide(1), whole((heads, inner)),
            pl.BlockSpec((1, width, inner), lambda i: (last - i, 0, 0)),
        ],
        out_specs=[
            tall(channels), whole((8, channels)), tall(heads), tall(heads), wide(heads),
            per_block, per_block,
        ],
        out_shape=[
            jax.ShapeDtypeStruct((rows, channels), jnp.bfloat16),
            jax.ShapeDtypeStruct((8, channels), f32),
            jax.ShapeDtypeStruct((rows, heads), f32),
            jax.ShapeDtypeStruct((rows, heads), f32),
            jax.ShapeDtypeStruct((heads, rows), f32),
            jax.ShapeDtypeStruct((t["count"], 1, inner), f32),
            jax.ShapeDtypeStruct((t["count"], 1, inner), f32),
        ],
        scratch_shapes=[
            pltpu.VMEM((width, inner), f32),
            pltpu.VMEM((BLOCK + 8, channels), f32),
            pltpu.VMEM((BLOCK + 16, channels), f32),
        ],
        compiler_params=pltpu.CompilerParams(vmem_limit_bytes=40 * 2**20),
        cost_estimate=pl.CostEstimate(
            flops=10 * 10**9, bytes_accessed=16 * 2**20, transcendentals=4 * 2**20
        ),
        name="scan_backward",
    )(
        act, u, u, dy, t["taps"], t["conv_bias"], t["joins"], t["nexts"], t["cum"], t["cum_r"], t["step_r"], t["early"], t["tail"], t["rest"],
        t["kept"], t["skip"], t["ids_c"], t["ids_r"], t["expand"], states,
    )
    count = t["count"]
    direct = col.T + late
    after = row - direct * t["step"]
    ends = jnp.sum((late * t["step"]).reshape(count, BLOCK, heads), axis=1)
    ends = ends + jnp.sum(keep.reshape(count, heads, -1), axis=2)
    d_decay = jnp.einsum(
        "ij,bih->bjh", t["lower"], after.reshape(count, BLOCK, heads), precision=HIGHEST
    )
    d_decay = (d_decay + ends[:, None, :]).reshape(rows, heads)
    d_step = direct + t["rate"] * d_decay
    d_logs = jnp.sum(d_decay * t["decay"], axis=0)
    d_skip = jnp.sum(dskip.reshape(count, heads, -1), axis=(0, 2))
    return du, conv, d_step, d_logs, d_skip


def swap(value, axis, bit):
    count = lax.axis_size(axis)
    return lax.ppermute(value, axis, [(i, i ^ bit) for i in range(count)])


def sum_all(value, axes):
    for axis in axes:
        bit = 1
        while bit < lax.axis_size(axis):
            value = value + swap(value, axis, bit)
            bit *= 2
    return value


def gather_rows(block):
    if lax.axis_size("tensor") != 4:
        return lax.all_gather(block, "tensor", axis=0, tiled=True)
    rows = block.shape[0]
    index = lax.axis_index("tensor")
    far = swap(block, "tensor", 2)
    near = swap(block, "tensor", 1)
    cross = swap(far, "tensor", 1)
    total = jnp.zeros((4 * rows, block.shape[1]), block.dtype)
    for bits, part in ((0, block), (1, near), (2, far), (3, cross)):
        total = put_slice(total, part, (index ^ bits) * rows, 0)
    return total


def scatter_rows(total):
    low = total.astype(jnp.bfloat16)
    if lax.axis_size("tensor") != 4:
        return lax.psum_scatter(low, "tensor", scatter_dimension=0, tiled=True).astype(jnp.float32)
    rows, cols = total.shape[0] // 4, total.shape[1]
    index = lax.axis_index("tensor")

    def block_of(value, place):
        return lax.dynamic_slice_in_dim(value, place * rows, rows, 0)

    def chip_sum(place):
        got = swap(block_of(low, place ^ 1), "tensor", 1)
        return block_of(low, place).astype(jnp.float32) + got.astype(jnp.float32)

    far = swap(chip_sum(index ^ 2).astype(jnp.bfloat16), "tensor", 2)
    return chip_sum(index) + far.astype(jnp.float32)


def local(
    residual,
    cotangent,
    seq_ids,
    w_zx,
    w_bc,
    w_dt,
    w_out,
    conv_weight,
    conv_bias,
    dt_bias,
    a_log,
    d_skip,
    norm_gain,
    pre_gain,
):
    tensor_index = lax.axis_index("tensor")
    own_rows = residual.shape[0]
    group_rows = seq_ids.shape[0]
    model_width = residual.shape[1]
    state_width = w_bc.shape[1] // 2
    heads_all = dt_bias.shape[0]
    inner_all = norm_gain.shape[0]
    head_dim = inner_all // heads_all
    margin = conv_weight.shape[0] - 1
    channels_all = conv_weight.shape[1]
    residual_f = residual.astype(jnp.float32)
    inv_rms = lax.rsqrt(jnp.mean(residual_f * residual_f, axis=1, keepdims=True) + EPSILON)
    normed = (residual_f * inv_rms * pre_gain).astype(jnp.bfloat16)
    dt_cols = w_dt.shape[1]
    w_in = lax.all_gather(
        jnp.concatenate([w_zx[:, 1], w_bc, w_dt], axis=1), "dp", axis=0, tiled=True
    )
    w_rest = lax.all_gather(
        jnp.concatenate([w_zx[:, 0], w_out.T], axis=1), "dp", axis=0, tiled=True
    )
    own_ids = lax.dynamic_slice_in_dim(seq_ids, tensor_index * own_rows, own_rows)
    live_rows = (own_ids >= 0).astype(jnp.float32)[:, None]
    grad_cot = cotangent * live_rows.astype(jnp.bfloat16)
    heads_here = dt_cols
    inner_here = heads_here * head_dim
    col_start = tensor_index * inner_here
    head_start = tensor_index * heads_here
    rows_normed = gather_rows(normed)
    cot_rows = gather_rows(grad_cot)
    channels_here = inner_here + 2 * state_width
    projected = jnp.dot(rows_normed, w_in, preferred_element_type=jnp.float32).astype(jnp.bfloat16)
    raw_f = projected[:, channels_here:].astype(jnp.float32)
    conv_w_here = jnp.concatenate(
        [
            lax.dynamic_slice_in_dim(conv_weight, col_start, inner_here, 1),
            conv_weight[:, inner_all:],
        ],
        axis=1,
    )
    conv_b_here = jnp.concatenate(
        [lax.dynamic_slice_in_dim(conv_bias, col_start, inner_here), conv_bias[inner_all:]]
    )
    dt_b_here = lax.dynamic_slice_in_dim(dt_bias, head_start, heads_here)
    logs_here = lax.dynamic_slice_in_dim(a_log, head_start, heads_here)
    skip_here = lax.dynamic_slice_in_dim(d_skip, head_start, heads_here)
    gain_here = lax.dynamic_slice_in_dim(norm_gain, col_start, inner_here)
    terms = scan_terms(
        raw_f, dt_b_here, logs_here, skip_here, seq_ids, inner_here, conv_w_here, conv_b_here
    )
    mixed, states, activated = scan_forward(projected, terms)
    mixed_f = mixed.astype(jnp.float32)
    w_gate, out_wt = w_rest[:, :inner_here], w_rest[:, inner_here:]
    gate_in = (
        jnp.dot(rows_normed, w_gate, preferred_element_type=jnp.float32)
        .astype(jnp.bfloat16)
        .astype(jnp.float32)
    )
    grad_branch = jnp.dot(cot_rows, out_wt, preferred_element_type=jnp.float32)
    weighted = grad_branch * gain_here
    gate_act = silu_of(gate_in)
    gated_rows = mixed_f * gate_act
    row_sums = jnp.stack(
        [jnp.sum(gated_rows * gated_rows, axis=1), jnp.sum(weighted * gated_rows, axis=1)]
    )
    sum_sq, dots_total = lax.psum(row_sums, "tensor")
    row_scale = lax.rsqrt(sum_sq / inner_all + EPSILON)[:, None]
    branch = (gated_rows * row_scale * gain_here).astype(jnp.bfloat16)
    grad_gated = (
        row_scale * weighted - gated_rows * row_scale**3 * (dots_total / inner_all)[:, None]
    )
    gain_local = jnp.sum(grad_branch * gated_rows * row_scale, axis=0)
    grad_mixed = (grad_gated * gate_act).astype(jnp.bfloat16)
    grad_gate = (grad_gated * mixed_f * silu_slope(gate_in)).astype(jnp.bfloat16)
    grad_rest = jnp.concatenate(
        [matmul_rows(rows_normed, grad_gate), matmul_rows(cot_rows, branch)], axis=1
    ).astype(jnp.bfloat16)
    mix_part = matmul_cols(branch, out_wt).astype(jnp.bfloat16)
    grad_mixed, grad_rest, mix_part = lax.optimization_barrier((grad_mixed, grad_rest, mix_part))
    grad_rest = lax.psum_scatter(grad_rest, "dp", scatter_dimension=0, tiled=True)
    output = residual_f + live_rows * scatter_rows(mix_part)
    grad_conv_in, grad_conv, grad_step, grad_logs, grad_skip = scan_backward(
        activated, projected, grad_mixed, states, terms
    )
    grad_conv_w, grad_conv_b = grad_conv[: margin + 1], grad_conv[margin + 1]
    grad_raw = grad_step * jax.nn.sigmoid(raw_f + dt_b_here)
    grad_dt_b = jnp.sum(grad_raw, axis=0)
    grad_in = jnp.concatenate([grad_conv_in, grad_raw.astype(jnp.bfloat16)], axis=1)
    grad_in_w = matmul_rows(rows_normed, grad_in).astype(jnp.bfloat16)
    grad_in_w = lax.psum_scatter(grad_in_w, "dp", scatter_dimension=0, tiled=True)
    normed_part = matmul_cols(grad_gate, w_gate) + matmul_cols(grad_in, w_in)
    grad_normed = scatter_rows(normed_part)
    grad_pre = jnp.sum(normed_part * rows_normed.astype(jnp.float32), axis=0) / pre_gain
    conv_w_full = jnp.zeros((margin + 1, channels_all), jnp.float32)
    conv_w_full = put_slice(conv_w_full, grad_conv_w[:, :inner_here], col_start, 1)
    conv_w_full = put_slice(conv_w_full, grad_conv_w[:, inner_here:], inner_all, 1)
    conv_b_full = jnp.zeros((channels_all,), jnp.float32)
    conv_b_full = put_slice(conv_b_full, grad_conv_b[:inner_here], col_start, 0)
    conv_b_full = put_slice(conv_b_full, grad_conv_b[inner_here:], inner_all, 0)
    dt_b_full = put_slice(jnp.zeros((heads_all,), jnp.float32), grad_dt_b, head_start, 0)
    logs_full = put_slice(jnp.zeros((heads_all,), jnp.float32), grad_logs, head_start, 0)
    skip_full = put_slice(jnp.zeros((heads_all,), jnp.float32), grad_skip, head_start, 0)
    gain_full = put_slice(jnp.zeros((inner_all,), jnp.float32), gain_local, col_start, 0)
    grad_residual = (
        cotangent.astype(jnp.float32)
        + inv_rms * pre_gain * grad_normed
        - residual_f
        * inv_rms**3
        * jnp.mean(grad_normed * pre_gain * residual_f, axis=1, keepdims=True)
    )
    grad_in_w = grad_in_w.astype(jnp.float32)
    grad_rest = grad_rest.astype(jnp.float32)
    grad_zx_w = jnp.stack([grad_rest[:, :inner_here], grad_in_w[:, :inner_here]], axis=1)
    grad_bc_w = sum_all(grad_in_w[:, inner_here:channels_here], ("tensor",))
    grad_dt_w = grad_in_w[:, channels_here:]
    grad_out_w = grad_rest[:, inner_here:].T
    small = [conv_w_full, conv_b_full, dt_b_full, logs_full, skip_full, gain_full, grad_pre]
    packed = jnp.concatenate([part.reshape(-1) for part in small])
    packed = sum_all(packed, ("tensor", "dp"))
    small_sums, first = [], 0
    for part in small:
        small_sums.append(packed[first : first + part.size].reshape(part.shape))
        first += part.size
    return (
        output,
        grad_residual,
        grad_zx_w,
        grad_bc_w,
        grad_dt_w,
        grad_out_w,
        small_sums[0],
        small_sums[1],
        small_sums[2],
        small_sums[3],
        small_sums[4],
        small_sums[5],
        small_sums[6],
    )


def solution(mesh):
    placed = (
        P(("dp", "tensor"), None),
        P(("dp", "tensor"), None),
        P("dp"),
        P("dp", None, "tensor"),
        P("dp", None),
        P("dp", "tensor"),
        P("tensor", "dp"),
        P(),
        P(),
        P(),
        P(),
        P(),
        P(),
        P(),
    )
    return jax.shard_map(
        local,
        mesh=mesh,
        in_specs=placed,
        out_specs=(
            P(("dp", "tensor"), None),
            P(("dp", "tensor"), None),
            P("dp", None, "tensor"),
            P("dp", None),
            P("dp", "tensor"),
            P("tensor", "dp"),
            P(),
            P(),
            P(),
            P(),
            P(),
            P(),
            P(),
        ),
        check_vma=False,
    )
```

```python
import jax
import jax.numpy as jnp
from jax import lax
from jax.experimental import pallas as pl
from jax.experimental.pallas import tpu as pltpu
from jax.experimental.layout import Layout, with_layout_constraint
from jax.sharding import PartitionSpec as P

BLOCK = 256


EPSILON = 1e-05
HIGHEST = lax.Precision.HIGHEST
CONTRACT_ROWS = (((0,), (0,)), ((), ()))
CONTRACT_COLS = (((1,), (1,)), ((), ()))


def silu_of(value):
    return value * jax.nn.sigmoid(value)


def silu_slope(value):
    sigmoid_val = jax.nn.sigmoid(value)
    return sigmoid_val * (1.0 + value * (1.0 - sigmoid_val))


def rounded(value):
    return lax.optimization_barrier(value.astype(jnp.bfloat16)).astype(jnp.float32)


def matmul_rows(left_mat, right_mat):
    return lax.dot_general(left_mat, right_mat, CONTRACT_ROWS, preferred_element_type=jnp.float32)


def matmul_cols(left_mat, right_mat):
    return lax.dot_general(left_mat, right_mat, CONTRACT_COLS, preferred_element_type=jnp.float32)


def put_slice(total_vec, piece_vec, first_index, axis_pos):
    return lax.dynamic_update_slice_in_dim(total_vec, piece_vec, first_index, axis_pos)


def dot_of(left_mat, right_mat, left_dim, right_dim):
    return lax.dot_general(
        left_mat,
        right_mat,
        (((left_dim,), (right_dim,)), ((), ())),
        preferred_element_type=jnp.float32,
    )


def spread(cols, expand):
    return jnp.dot(cols, expand, precision=HIGHEST, preferred_element_type=jnp.float32)


def head_decay(cum_c, cum_r, mask, head):
    gap = jnp.where(mask, cum_c[:, head : head + 1] - cum_r[head : head + 1, :], -1e30)
    return jnp.exp(gap)


def block_mask(id_c, id_r):
    size = id_c.shape[0]
    row = lax.broadcasted_iota(jnp.int32, (size, size), 0)
    col = lax.broadcasted_iota(jnp.int32, (size, size), 1)
    return (row >= col) & (id_c == id_r)


def pair_masks(size, width, heads):
    lane = lax.broadcasted_iota(jnp.int32, (size, width), 1)
    part = width // heads
    return [(lane // part) == k for k in range(heads)]


def forward_kernel(
    u_ref, taps_ref, bias_ref, joins_ref, cumc_ref, cumr_ref, dtr_ref, ec_ref, tail_ref, kept_ref,
    skip_ref, idc_ref, idr_ref, expand_ref, y_ref, h_ref, act_ref, state, ext,
):
    heads = cumc_ref.shape[1]
    size, inner = y_ref.shape
    width = (u_ref.shape[1] - inner) // 2
    per = 128 * heads // inner

    @pl.when(pl.program_id(0) == 0)
    def _():
        state[...] = jnp.zeros_like(state)
        ext[size : size + 8, :] = jnp.zeros((8, ext.shape[1]), jnp.float32)

    expand = expand_ref[...]
    joins = joins_ref[...]
    ext[0:8, :] = ext[size : size + 8, :]
    ext[8 : size + 8, :] = u_ref[...].astype(jnp.float32)
    for first in range(0, u_ref.shape[1], 128):
        lanes = slice(first, first + 128)
        pre = bias_ref[:, lanes] + taps_ref[0:1, lanes] * ext[8 : size + 8, lanes]
        for k in range(1, taps_ref.shape[0]):
            shifted = ext[8 - k : size + 8 - k, lanes] * joins[:, k - 1 : k]
            pre = pre + taps_ref[k : k + 1, lanes] * shifted
        act_ref[:, lanes] = silu_of(pre).astype(act_ref.dtype)
    x = act_ref[:, :inner]
    b = act_ref[:, inner : inner + width]
    c = act_ref[:, inner + width :]
    h_low = state[...].astype(jnp.bfloat16)
    h_ref[0] = h_low
    x_f = x.astype(jnp.float32)
    y_all = dot_of(c, h_low, 1, 0) * spread(ec_ref[...], expand) + skip_ref[...] * x_f
    scores = dot_of(c, b, 1, 1)
    mask = block_mask(idc_ref[...], idr_ref[...])
    cum_c, cum_r, dt_r = cumc_ref[...], cumr_ref[...], dtr_ref[...]
    sides = pair_masks(size, 128, per)
    for pair in range(heads // per):
        lanes = slice(128 * pair, 128 * pair + 128)
        x_pair = x[:, lanes]
        acc = y_all[:, lanes]
        for k in range(per):
            head = pair * per + k
            mix = scores * head_decay(cum_c, cum_r, mask, head) * dt_r[head : head + 1, :]
            part = jnp.where(sides[k], x_pair, jnp.zeros_like(x_pair))
            acc = acc + dot_of(mix.astype(jnp.bfloat16), part, 1, 0)
        y_ref[:, lanes] = acc.astype(y_ref.dtype)
    tail = spread(tail_ref[...], expand)
    state[...] = state[...] * kept_ref[0] + dot_of(b, (x_f * tail).astype(jnp.bfloat16), 0, 0)


def backward_kernel(
    act_ref, u_ref, past_ref, dy_ref, taps_ref, bias_ref, joins_ref, nexts_ref,
    cumc_ref, cumr_ref, dtr_ref, ec_ref, tail_ref, rate_ref,
    kept_ref, skip_ref, idc_ref, idr_ref, expand_ref, h_ref,
    du_ref, conv_ref, row_ref, late_ref, col_ref, keep_ref, dskip_ref, grad, ext, past,
):
    heads = cumc_ref.shape[1]
    size, inner = dy_ref.shape
    width = (u_ref.shape[1] - inner) // 2
    tap_count = taps_ref.shape[0]
    per = 128 * heads // inner

    @pl.when(pl.program_id(0) == 0)
    def _():
        grad[...] = jnp.zeros_like(grad)
        conv_ref[...] = jnp.zeros_like(conv_ref)
        ext[0:8, :] = jnp.zeros((8, ext.shape[1]), jnp.float32)

    ext[size : size + 8, :] = ext[0:8, :]
    past[0:16, :] = past_ref[...].astype(jnp.float32)
    past[16 : size + 16, :] = u_ref[...].astype(jnp.float32)
    expand = expand_ref[...]
    dy, h_low = dy_ref[...], h_ref[0]
    x = act_ref[:, :inner]
    b = act_ref[:, inner : inner + width]
    c = act_ref[:, inner + width :]
    x_f, dy_f = x.astype(jnp.float32), dy.astype(jnp.float32)
    g_now = grad[...]
    g_low = g_now.astype(jnp.bfloat16)
    early = spread(ec_ref[...], expand)
    tail = spread(tail_ref[...], expand)
    dy_early = dy_f * early
    dy_early_low = dy_early.astype(jnp.bfloat16)
    from_state = dot_of(c, h_low, 1, 0)
    to_state = dot_of(b, g_low, 1, 0)

    def by_head(value):
        return lax.dot_general(
            value, expand, CONTRACT_COLS, precision=HIGHEST, preferred_element_type=jnp.float32
        )

    late_ref[...] = by_head(x_f * to_state) * rate_ref[...]
    row_sums = by_head(dy_early * from_state)
    keep_ref[0] = jnp.sum(h_low.astype(jnp.float32) * g_now, axis=0, keepdims=True) * kept_ref[0]
    dskip_ref[0] = jnp.sum(x_f * dy_f, axis=0, keepdims=True)
    grad[...] = g_now * kept_ref[0] + dot_of(c, dy_early_low, 0, 0)
    dx_all = skip_ref[...] * dy_f + tail * to_state
    scores = dot_of(c, b, 1, 1)
    mask = block_mask(idc_ref[...], idr_ref[...])
    cum_c, cum_r, dt_r = cumc_ref[...], cumr_ref[...], dtr_ref[...]
    sides = pair_masks(size, 128, per)
    head_lane = lax.broadcasted_iota(jnp.int32, (size, heads), 1)
    d_scores = jnp.zeros((size, size), jnp.float32)
    for pair in range(heads // per):
        lanes = slice(128 * pair, 128 * pair + 128)
        x_pair, dy_pair = x[:, lanes], dy[:, lanes]
        acc = dx_all[:, lanes]
        for k in range(per):
            head = pair * per + k
            decay = head_decay(cum_c, cum_r, mask, head)
            dt_row = dt_r[head : head + 1, :]
            dy_part = jnp.where(sides[k], dy_pair, jnp.zeros_like(dy_pair))
            d_mix = dot_of(dy_part, x_pair, 1, 1) * decay
            d_scores = d_scores + d_mix * dt_row
            core = d_mix * scores
            col_ref[head : head + 1, :] = jnp.sum(core, axis=0, keepdims=True)
            row_sum = jnp.sum(core * dt_row, axis=1, keepdims=True)
            row_sums = row_sums + jnp.where(head_lane == head, row_sum, 0.0)
            mix = (scores * decay * dt_row).astype(jnp.bfloat16)
            acc = acc + dot_of(mix, dy_part, 0, 0)
        ext[0:size, lanes] = acc
    row_ref[...] = row_sums
    d_low = d_scores.astype(jnp.bfloat16)
    x_tail = (x_f * tail).astype(jnp.bfloat16)
    ext[0:size, inner : inner + width] = dot_of(d_low, c, 0, 0) + dot_of(x_tail, g_low, 1, 1)
    ext[0:size, inner + width :] = dot_of(d_low, b, 1, 0) + dot_of(dy_early_low, h_low, 1, 1)
    joins, nexts = joins_ref[...], nexts_ref[...]
    for first in range(0, u_ref.shape[1], 128):
        lanes = slice(first, first + 128)
        moved = [past[16 : size + 16, lanes]]
        for k in range(1, tap_count):
            moved.append(past[16 - k : size + 16 - k, lanes] * joins[:, k - 1 : k])
        pre = bias_ref[:, lanes]
        for k in range(tap_count):
            pre = pre + taps_ref[k : k + 1, lanes] * moved[k]
        d_pre = ext[0:size, lanes] * silu_slope(pre)
        ext[0:size, lanes] = d_pre
        for k in range(tap_count):
            conv_ref[k : k + 1, lanes] += jnp.sum(d_pre * moved[k], axis=0, keepdims=True)
        conv_ref[tap_count : tap_count + 1, lanes] += jnp.sum(d_pre, axis=0, keepdims=True)
        du = taps_ref[0:1, lanes] * d_pre
        for k in range(1, tap_count):
            later = ext[k : size + k, lanes] * nexts[:, k - 1 : k]
            du = du + taps_ref[k : k + 1, lanes] * later
        du_ref[:, lanes] = du.astype(du_ref.dtype)


def scan_terms(raw_rates, bias_vec, log_rates, skip_gain, ids, inner, taps, conv_bias):
    rows, heads = raw_rates.shape
    count = rows // BLOCK
    step = jax.nn.softplus(raw_rates + bias_vec)
    rate = -jnp.exp(log_rates)
    decay = rate * step
    lower = (jnp.arange(BLOCK)[:, None] >= jnp.arange(BLOCK)[None, :]).astype(jnp.float32)
    cum = jnp.einsum(
        "ij,bjh->bih", lower, decay.reshape(count, BLOCK, heads), precision=HIGHEST
    )
    blocks = ids.reshape(count, BLOCK)
    before = jnp.concatenate([jnp.full((1,), -2, ids.dtype), blocks[:-1, -1]])
    joins = (blocks == before[:, None])[:, :, None]
    stays = (blocks == blocks[:, -1:])[:, :, None]
    early = jnp.where(joins, jnp.exp(cum), 0.0)
    rest = jnp.where(stays, jnp.exp(cum[:, -1:] - cum), 0.0)
    tail = rest * step.reshape(count, BLOCK, heads)
    part = inner // heads
    kept = jnp.repeat(early[:, -1:], part, axis=2)
    expand = jnp.repeat(jnp.eye(heads, dtype=jnp.float32), part, axis=1)

    joins, nexts = [], []
    for k in range(1, taps.shape[0]):
        same = (ids[k:] == ids[:-k]).astype(jnp.float32)
        joins.append(jnp.pad(same, (k, 0)))
        nexts.append(jnp.pad(same, (0, k)))

    def flat(value):
        return value.reshape(rows, heads)

    return dict(
        step=step, decay=decay, rate=rate, lower=lower, count=count, kept=kept, expand=expand,
        cum=flat(cum), cum_r=flat(cum).T, step_r=step.T, early=flat(early), rest=flat(rest),
        tail=flat(tail), skip=jnp.repeat(skip_gain, part)[None, :],
        ids_c=ids[:, None], ids_r=ids[None, :], joins=jnp.stack(joins, axis=1),
        nexts=jnp.stack(nexts, axis=1), taps=taps, conv_bias=conv_bias[None, :],
    )


def scan_forward(u, t):
    rows, heads = t["cum"].shape
    inner = t["expand"].shape[1]
    channels = t["taps"].shape[1]
    width = (channels - inner) // 2
    shifts = t["joins"].shape[1]

    def tall(cols):
        return pl.BlockSpec((BLOCK, cols), lambda i: (i, 0))

    def wide(rows_):
        return pl.BlockSpec((rows_, BLOCK), lambda i: (0, i))

    def whole(shape):
        return pl.BlockSpec(shape, lambda i: (0, 0))

    per_block = pl.BlockSpec((1, 1, inner), lambda i: (i, 0, 0))
    return pl.pallas_call(
        forward_kernel,
        grid=(t["count"],),
        in_specs=[
            tall(channels), whole(t["taps"].shape), whole((1, channels)), tall(shifts),
            tall(heads), wide(heads), wide(heads), tall(heads), tall(heads), per_block,
            whole((1, inner)), tall(1), wide(1), whole((heads, inner)),
        ],
        out_specs=[
            tall(inner),
            pl.BlockSpec((1, width, inner), lambda i: (i, 0, 0)),
            tall(channels),
        ],
        out_shape=[
            jax.ShapeDtypeStruct((rows, inner), jnp.bfloat16),
            jax.ShapeDtypeStruct((t["count"], width, inner), jnp.bfloat16),
            jax.ShapeDtypeStruct((rows, channels), jnp.bfloat16),
        ],
        scratch_shapes=[
            pltpu.VMEM((width, inner), jnp.float32),
            pltpu.VMEM((BLOCK + 8, channels), jnp.float32),
        ],
        compiler_params=pltpu.CompilerParams(vmem_limit_bytes=40 * 2**20),
        cost_estimate=pl.CostEstimate(
            flops=4 * 10**9, bytes_accessed=8 * 2**20, transcendentals=4 * 2**20
        ),
        name="scan_forward",
    )(
        u, t["taps"], t["conv_bias"], t["joins"], t["cum"], t["cum_r"], t["step_r"], t["early"],
        t["tail"], t["kept"], t["skip"], t["ids_c"], t["ids_r"], t["expand"],
    )


def after_kernel(value_ref, first_ref, other_ref, out_ref):
    out_ref[...] = value_ref[...]


def wait_for(value, first, other):
    return pl.pallas_call(
        after_kernel,
        in_specs=[pl.BlockSpec(memory_space=pltpu.VMEM)] + [pl.BlockSpec(memory_space=pl.ANY)] * 2,
        out_specs=pl.BlockSpec(memory_space=pltpu.VMEM),
        out_shape=jax.ShapeDtypeStruct(value.shape, value.dtype),
        compiler_params=pltpu.CompilerParams(vmem_limit_bytes=2**20),
        name="after",
    )(value, first, other)


def scan_backward(act, u, dy, states, t, earlier):
    rows, heads = t["cum"].shape
    inner = t["expand"].shape[1]
    channels = t["taps"].shape[1]
    width = (channels - inner) // 2
    shifts = t["joins"].shape[1]
    last = t["count"] - 1

    def tall(cols):
        return pl.BlockSpec((BLOCK, cols), lambda i: (last - i, 0))

    def wide(rows_):
        return pl.BlockSpec((rows_, BLOCK), lambda i: (0, last - i))

    def whole(shape):
        return pl.BlockSpec(shape, lambda i: (0, 0))

    per_block = pl.BlockSpec((1, 1, inner), lambda i: (last - i, 0, 0))
    f32 = jnp.float32
    du, conv, row, late, col, keep, dskip = pl.pallas_call(
        backward_kernel,
        grid=(t["count"],),
        in_specs=[
            tall(channels), tall(channels),
            pl.BlockSpec(
                (16, channels), lambda i: (jnp.maximum((last - i) * (BLOCK // 16) - 1, 0), 0)
            ),
            tall(inner), whole(t["taps"].shape), whole((1, channels)), tall(shifts), tall(shifts),
            tall(heads), wide(heads),
            wide(heads), tall(heads), tall(heads), tall(heads), per_block, whole((1, inner)),
            tall(1), wide(1), whole((heads, inner)),
            pl.BlockSpec((1, width, inner), lambda i: (last - i, 0, 0)),
        ],
        out_specs=[
            tall(channels), whole((8, channels)), tall(heads), tall(heads), wide(heads),
            per_block, per_block,
        ],
        out_shape=[
            jax.ShapeDtypeStruct((rows, channels), jnp.bfloat16),
            jax.ShapeDtypeStruct((8, channels), f32),
            jax.ShapeDtypeStruct((rows, heads), f32),
            jax.ShapeDtypeStruct((rows, heads), f32),
            jax.ShapeDtypeStruct((heads, rows), f32),
            jax.ShapeDtypeStruct((t["count"], 1, inner), f32),
            jax.ShapeDtypeStruct((t["count"], 1, inner), f32),
        ],
        scratch_shapes=[
            pltpu.VMEM((width, inner), f32),
            pltpu.VMEM((BLOCK + 8, channels), f32),
            pltpu.VMEM((BLOCK + 16, channels), f32),
        ],
        compiler_params=pltpu.CompilerParams(vmem_limit_bytes=40 * 2**20),
        cost_estimate=pl.CostEstimate(
            flops=10 * 10**9, bytes_accessed=16 * 2**20, transcendentals=4 * 2**20
        ),
        name="scan_backward",
    )(
        act, u, u, dy, t["taps"], t["conv_bias"], t["joins"], t["nexts"], t["cum"], t["cum_r"], t["step_r"], t["early"], t["tail"], t["rest"],
        t["kept"], t["skip"], t["ids_c"], t["ids_r"], t["expand"], states,
    )
    count = t["count"]
    direct = wait_for(col, *earlier).T + late
    after = row - direct * t["step"]
    ends = jnp.sum((late * t["step"]).reshape(count, BLOCK, heads), axis=1)
    ends = ends + jnp.sum(keep.reshape(count, heads, -1), axis=2)
    d_decay = jnp.einsum(
        "ij,bih->bjh", t["lower"], after.reshape(count, BLOCK, heads), precision=HIGHEST
    )
    d_decay = (d_decay + ends[:, None, :]).reshape(rows, heads)
    d_step = direct + t["rate"] * d_decay
    d_logs = jnp.sum(d_decay * t["decay"], axis=0)
    d_skip = jnp.sum(dskip.reshape(count, heads, -1), axis=(0, 2))
    return du, conv, d_step, d_logs, d_skip


def swap(value, axis, bit):
    count = lax.axis_size(axis)
    return lax.ppermute(value, axis, [(i, i ^ bit) for i in range(count)])


def sum_all(value, axes):
    for axis in axes:
        bit = 1
        while bit < lax.axis_size(axis):
            value = value + swap(value, axis, bit)
            bit *= 2
    return value


def row_major(value):
    return with_layout_constraint(value, Layout(major_to_minor=(0, 1)))


def scatter_dp(total):
    count = lax.axis_size("dp")
    bits = count.bit_length() - 1
    if 1 << bits != count:
        return lax.psum_scatter(total, "dp", scatter_dimension=0, tiled=True).astype(jnp.float32)
    index = lax.axis_index("dp")
    left = list(range(bits - 1, -1, -1))
    value = total.reshape((2,) * bits + (total.shape[0] // count, total.shape[1]))
    for bit in [0] + list(range(bits - 1, 0, -1)):
        place = left.index(bit)
        mine = (index >> bit) & 1
        keep = lax.dynamic_index_in_dim(value, mine, place, keepdims=False)
        send = lax.dynamic_index_in_dim(value, 1 - mine, place, keepdims=False)
        got = swap(send.astype(jnp.bfloat16), "dp", 1 << bit)
        value = keep.astype(jnp.float32) + got.astype(jnp.float32)
        left.remove(bit)
    return value


def gather_rows(block):
    if lax.axis_size("tensor") != 4:
        return lax.all_gather(block, "tensor", axis=0, tiled=True)
    rows = block.shape[0]
    index = lax.axis_index("tensor")
    far = swap(block, "tensor", 2)
    near = swap(block, "tensor", 1)
    cross = swap(far, "tensor", 1)
    total = jnp.zeros((4 * rows, block.shape[1]), block.dtype)
    for bits, part in ((0, block), (1, near), (2, far), (3, cross)):
        total = put_slice(total, part, (index ^ bits) * rows, 0)
    return total


def scatter_rows(total):
    low = total.astype(jnp.bfloat16)
    if lax.axis_size("tensor") != 4:
        return lax.psum_scatter(low, "tensor", scatter_dimension=0, tiled=True).astype(jnp.float32)
    rows, cols = total.shape[0] // 4, total.shape[1]
    index = lax.axis_index("tensor")

    def block_of(value, place):
        return lax.dynamic_slice_in_dim(value, place * rows, rows, 0)

    def chip_sum(place):
        got = swap(block_of(low, place ^ 1), "tensor", 1)
        return block_of(low, place).astype(jnp.float32) + got.astype(jnp.float32)

    far = swap(chip_sum(index ^ 2).astype(jnp.bfloat16), "tensor", 2)
    return chip_sum(index) + far.astype(jnp.float32)


def local(
    residual,
    cotangent,
    seq_ids,
    w_zx,
    w_bc,
    w_dt,
    w_out,
    conv_weight,
    conv_bias,
    dt_bias,
    a_log,
    d_skip,
    norm_gain,
    pre_gain,
):
    tensor_index = lax.axis_index("tensor")
    own_rows = residual.shape[0]
    group_rows = seq_ids.shape[0]
    model_width = residual.shape[1]
    state_width = w_bc.shape[1] // 2
    heads_all = dt_bias.shape[0]
    inner_all = norm_gain.shape[0]
    head_dim = inner_all // heads_all
    margin = conv_weight.shape[0] - 1
    channels_all = conv_weight.shape[1]
    residual_f = residual.astype(jnp.float32)
    inv_rms = lax.rsqrt(jnp.mean(residual_f * residual_f, axis=1, keepdims=True) + EPSILON)
    normed = (residual_f * inv_rms * pre_gain).astype(jnp.bfloat16)
    dt_cols = w_dt.shape[1]
    w_in = lax.all_gather(
        jnp.concatenate([w_zx[:, 1], w_bc, w_dt], axis=1), "dp", axis=0, tiled=True
    )
    w_rest = lax.all_gather(
        jnp.concatenate([w_zx[:, 0], w_out.T], axis=1), "dp", axis=0, tiled=True
    )
    own_ids = lax.dynamic_slice_in_dim(seq_ids, tensor_index * own_rows, own_rows)
    live_rows = (own_ids >= 0).astype(jnp.float32)[:, None]
    grad_cot = cotangent * live_rows.astype(jnp.bfloat16)
    heads_here = dt_cols
    inner_here = heads_here * head_dim
    col_start = tensor_index * inner_here
    head_start = tensor_index * heads_here
    rows_normed = gather_rows(normed)
    rows_normed, grad_cot = lax.optimization_barrier((rows_normed, grad_cot))
    cot_rows = gather_rows(grad_cot)
    channels_here = inner_here + 2 * state_width
    projected = row_major(
        jnp.dot(rows_normed, w_in[:, :channels_here], preferred_element_type=jnp.float32).astype(
            jnp.bfloat16
        )
    )
    raw_f = (
        jnp.dot(rows_normed, w_in[:, channels_here:], preferred_element_type=jnp.float32)
        .astype(jnp.bfloat16)
        .astype(jnp.float32)
    )
    conv_w_here = jnp.concatenate(
        [
            lax.dynamic_slice_in_dim(conv_weight, col_start, inner_here, 1),
            conv_weight[:, inner_all:],
        ],
        axis=1,
    )
    conv_b_here = jnp.concatenate(
        [lax.dynamic_slice_in_dim(conv_bias, col_start, inner_here), conv_bias[inner_all:]]
    )
    dt_b_here = lax.dynamic_slice_in_dim(dt_bias, head_start, heads_here)
    logs_here = lax.dynamic_slice_in_dim(a_log, head_start, heads_here)
    skip_here = lax.dynamic_slice_in_dim(d_skip, head_start, heads_here)
    gain_here = lax.dynamic_slice_in_dim(norm_gain, col_start, inner_here)
    terms = scan_terms(
        raw_f, dt_b_here, logs_here, skip_here, seq_ids, inner_here, conv_w_here, conv_b_here
    )
    mixed, states, activated = scan_forward(projected, terms)
    mixed_f = mixed.astype(jnp.float32)
    w_gate, out_wt = w_rest[:, :inner_here], w_rest[:, inner_here:]
    gate_in = (
        jnp.dot(rows_normed, w_gate, preferred_element_type=jnp.float32)
        .astype(jnp.bfloat16)
        .astype(jnp.float32)
    )
    grad_branch = jnp.dot(cot_rows, out_wt, preferred_element_type=jnp.float32)
    weighted = grad_branch * gain_here
    gate_act = silu_of(gate_in)
    gated_rows = mixed_f * gate_act
    row_sums = jnp.stack(
        [jnp.sum(gated_rows * gated_rows, axis=1), jnp.sum(weighted * gated_rows, axis=1)]
    )
    sum_sq, dots_total = lax.psum(row_sums, "tensor")
    row_scale = lax.rsqrt(sum_sq / inner_all + EPSILON)[:, None]
    branch = (gated_rows * row_scale * gain_here).astype(jnp.bfloat16)
    grad_gated = (
        row_scale * weighted - gated_rows * row_scale**3 * (dots_total / inner_all)[:, None]
    )
    gain_local = jnp.sum(grad_branch * gated_rows * row_scale, axis=0)
    grad_mixed = (grad_gated * gate_act).astype(jnp.bfloat16)
    grad_gate = (grad_gated * mixed_f * silu_slope(gate_in)).astype(jnp.bfloat16)
    grad_out = row_major(matmul_rows(cot_rows, branch).astype(jnp.bfloat16))
    grad_z = row_major(matmul_rows(rows_normed, grad_gate).astype(jnp.bfloat16))
    mix_part = matmul_cols(branch, out_wt).astype(jnp.bfloat16)
    grad_mixed, grad_out, grad_z, mix_part = lax.optimization_barrier(
        (grad_mixed, grad_out, grad_z, mix_part)
    )
    grad_out = lax.psum_scatter(grad_out, "dp", scatter_dimension=0, tiled=True)
    grad_z = lax.psum_scatter(grad_z, "dp", scatter_dimension=0, tiled=True)
    mix_rows = scatter_rows(mix_part)
    grad_conv_in, grad_conv, grad_step, grad_logs, grad_skip = scan_backward(
        activated, projected, grad_mixed, states, terms, (grad_out, mix_rows)
    )
    output = residual_f + live_rows * mix_rows
    grad_conv_w, grad_conv_b = grad_conv[: margin + 1], grad_conv[margin + 1]
    grad_raw = grad_step * jax.nn.sigmoid(raw_f + dt_b_here)
    grad_dt_b = jnp.sum(grad_raw, axis=0)
    grad_in = jnp.concatenate([grad_conv_in, grad_raw.astype(jnp.bfloat16)], axis=1)
    grad_in_w = row_major(matmul_rows(rows_normed, grad_in).astype(jnp.bfloat16))
    grad_in_w, grad_in = lax.optimization_barrier((grad_in_w, grad_in))
    grad_in_w = scatter_dp(grad_in_w)
    normed_part = matmul_cols(grad_gate, w_gate) + matmul_cols(grad_in, w_in)
    grad_normed = scatter_rows(normed_part)
    grad_pre = jnp.sum(normed_part * rows_normed.astype(jnp.float32), axis=0) / pre_gain
    conv_w_full = jnp.zeros((margin + 1, channels_all), jnp.float32)
    conv_w_full = put_slice(conv_w_full, grad_conv_w[:, :inner_here], col_start, 1)
    conv_w_full = put_slice(conv_w_full, grad_conv_w[:, inner_here:], inner_all, 1)
    conv_b_full = jnp.zeros((channels_all,), jnp.float32)
    conv_b_full = put_slice(conv_b_full, grad_conv_b[:inner_here], col_start, 0)
    conv_b_full = put_slice(conv_b_full, grad_conv_b[inner_here:], inner_all, 0)
    dt_b_full = put_slice(jnp.zeros((heads_all,), jnp.float32), grad_dt_b, head_start, 0)
    logs_full = put_slice(jnp.zeros((heads_all,), jnp.float32), grad_logs, head_start, 0)
    skip_full = put_slice(jnp.zeros((heads_all,), jnp.float32), grad_skip, head_start, 0)
    gain_full = put_slice(jnp.zeros((inner_all,), jnp.float32), gain_local, col_start, 0)
    grad_residual = (
        cotangent.astype(jnp.float32)
        + inv_rms * pre_gain * grad_normed
        - residual_f
        * inv_rms**3
        * jnp.mean(grad_normed * pre_gain * residual_f, axis=1, keepdims=True)
    )
    grad_z = grad_z.astype(jnp.float32)
    grad_zx_w = jnp.stack([grad_z, grad_in_w[:, :inner_here]], axis=1)
    grad_bc_w = sum_all(grad_in_w[:, inner_here:channels_here], ("tensor",))
    grad_dt_w = grad_in_w[:, channels_here:]
    grad_out_w = grad_out.astype(jnp.float32).T
    small = [conv_w_full, conv_b_full, dt_b_full, logs_full, skip_full, gain_full, grad_pre]
    packed = jnp.concatenate([part.reshape(-1) for part in small])
    packed = sum_all(packed, ("tensor", "dp"))
    small_sums, first = [], 0
    for part in small:
        small_sums.append(packed[first : first + part.size].reshape(part.shape))
        first += part.size
    return (
        output,
        grad_residual,
        grad_zx_w,
        grad_bc_w,
        grad_dt_w,
        grad_out_w,
        small_sums[0],
        small_sums[1],
        small_sums[2],
        small_sums[3],
        small_sums[4],
        small_sums[5],
        small_sums[6],
    )


def solution(mesh):
    placed = (
        P(("dp", "tensor"), None),
        P(("dp", "tensor"), None),
        P("dp"),
        P("dp", None, "tensor"),
        P("dp", None),
        P("dp", "tensor"),
        P("tensor", "dp"),
        P(),
        P(),
        P(),
        P(),
        P(),
        P(),
        P(),
    )
    return jax.shard_map(
        local,
        mesh=mesh,
        in_specs=placed,
        out_specs=(
            P(("dp", "tensor"), None),
            P(("dp", "tensor"), None),
            P("dp", None, "tensor"),
            P("dp", None),
            P("dp", "tensor"),
            P("tensor", "dp"),
            P(),
            P(),
            P(),
            P(),
            P(),
            P(),
            P(),
        ),
        check_vma=False,
    )
```
